32 devices in a mesh: lat: 8 (over y, x, core), lon: 4 (over z).
Axes of the slice: x: 2, y: 2, z: 4, core: 2. Of those that a mesh axis runs over, the one named last changes fastest.
Arguments:
- species_density: float32 [128, 1, 32, 512], P(None, None, 'lat', 'lon'), may hold values from 0.1 to 2
- zonal_wall_ratio: float32 [1, 32, 512], P(None, 'lat', 'lon'), may hold values from -0.4 to 0.4
- meridional_wall_ratio: float32 [1, 32, 512], P(None, 'lat', 'lon'), may hold values from -0.4 to 0.4
- normalized_warmth: float32 [1, 32, 512], P(None, 'lat', 'lon'), may hold values from -1 to 1
- kinetic_coefficient: float32 [512], replicated, may hold values from 0.05 to 1
- thermal_exponent: float32 [512], replicated, may hold values from -1 to 1
- product_amounts: float32 [512, 128], replicated, may hold values from 0 to 0.04
- reagent_pairs: int32 [2, 512], replicated, may hold values from 0 to 127
- inner_iterations: int32 [1, 32, 4], P(None, 'lat', 'lon'), may hold values from 1 to 4, as said below
- smoothed_parallel_flags: int32 [32], P('lat'), may hold values from 0 to 1, as said below
Outputs:
- tracer_out: float32 [128, 1, 32, 512], P(None, None, 'lat', 'lon')
The draws below stay inside these ranges and needn't reach their ends.
Inputs may be any that keep to these rules, and one draw needn't show every extreme that they name: `inner_iterations`: every block takes 1 substep except the blocks of one band of 4 consecutive latitude rows, which take 3 or 4. `smoothed_parallel_flags`: 1 on the first W1 and the last W2 latitude rows and 0 between them, for some W1 and W2 each from 1 to 8.
All inputs are finite; a program needn't handle non-finite values.
Results may differ from the reference program's by a relative error of at most 0.0003.
Values sent between devices are 32-bit elements; how exact they have to be, the bound alone decides.
A program may use at most 64 MiB of HBM per device.

```python
import math
import jax
import jax.numpy as jnp
from jax import lax

SPEC = 128
REAC = 512
MERIDIAN_PORTION = 128
VERTICAL_LAYERS = 1
ITERS = 2
PARALLEL_CIRCLES = 32
MERIDIAN_TOTAL = 512
N_LON = 4


def draw_inner_iterations(key, part):
    band_key, level_key = jax.random.split(jax.random.fold_in(key, 11))
    band_rows = PARALLEL_CIRCLES // 8
    band_start = jax.random.randint(band_key, (), 0, PARALLEL_CIRCLES - band_rows + 1)
    rows_index = jnp.arange(PARALLEL_CIRCLES)[None, :, None]
    inside = (rows_index >= band_start) & (rows_index < band_start + band_rows)
    heavy = 3 + jax.random.randint(level_key, (VERTICAL_LAYERS, PARALLEL_CIRCLES, N_LON), 0, 2)
    counts = jnp.where(inside, heavy, 1)
    marked = (jnp.arange(VERTICAL_LAYERS)[:, None, None] == 0) & (rows_index == band_start) & (jnp.arange(N_LON)[None, None, :] == 0)
    return jnp.where(marked, 4, counts).astype(jnp.int32)


def draw_smoothed_parallel_flags(key, part):
    rows_index = jnp.arange(PARALLEL_CIRCLES)
    most_width = max(1, PARALLEL_CIRCLES // 4)
    south_key, north_key = jax.random.split(jax.random.fold_in(key, 23))
    south_width = jax.random.randint(south_key, (), 1, most_width + 1)
    north_width = jax.random.randint(north_key, (), 1, most_width + 1)
    return jnp.where((rows_index < south_width) | (rows_index >= PARALLEL_CIRCLES - north_width), 1, 0).astype(jnp.int32)


def place_ends(result, stream_key, low, largest):
    longest = result.shape.index(max(result.shape))
    spots = []
    for shift in (0, 1):
        where = [jax.random.randint(jax.random.fold_in(stream_key, axis), (), 0, length) for axis, length in enumerate(result.shape)]
        where[longest] = (where[longest] + shift) % result.shape[longest]
        spots.append(tuple(where))
    return result.at[spots[0]].set(low).at[spots[1]].set(largest)


def shard_levels(own_key, shape, cuts, low, largest):
    def one(position, parts):
        steps = jax.random.uniform(jax.random.fold_in(jax.random.fold_in(own_key, 6), position), (parts,), jnp.float32, low / len(cuts), largest / len(cuts))
        return jnp.repeat(jnp.exp(steps), shape[position] // parts).reshape((-1,) + (1,) * (len(shape) - position - 1))

    factor_of = one(*cuts[0])
    for cut in cuts[1:]:
        factor_of = factor_of * one(*cut)
    return factor_of


def setup_inputs(seed: int = 0) -> dict:
    splits = jax.random.split(jax.random.key(seed), 11)
    return {
        "species_density": jnp.clip(jnp.exp(math.log(2.0) - 2.9957323 * jax.random.uniform(splits[0], (SPEC, VERTICAL_LAYERS, PARALLEL_CIRCLES, MERIDIAN_TOTAL), jnp.float32) ** shard_levels(splits[0], (SPEC, VERTICAL_LAYERS, PARALLEL_CIRCLES, MERIDIAN_TOTAL), ((2, 8), (3, 4)), -0.2, 0.2)), 0.1, 2.0),
        "zonal_wall_ratio": jnp.clip(jax.random.uniform(splits[1], (VERTICAL_LAYERS, PARALLEL_CIRCLES, MERIDIAN_TOTAL), jnp.float32, -0.4, 0.4) * shard_levels(splits[1], (VERTICAL_LAYERS, PARALLEL_CIRCLES, MERIDIAN_TOTAL), ((1, 8), (2, 4)), -0.4, 0.0), -0.4, 0.4),
        "meridional_wall_ratio": jnp.clip(jax.random.uniform(splits[2], (VERTICAL_LAYERS, PARALLEL_CIRCLES, MERIDIAN_TOTAL), jnp.float32, -0.4, 0.4) * shard_levels(splits[2], (VERTICAL_LAYERS, PARALLEL_CIRCLES, MERIDIAN_TOTAL), ((1, 8), (2, 4)), -0.4, 0.0), -0.4, 0.4),
        "normalized_warmth": jnp.clip(jax.random.uniform(splits[3], (VERTICAL_LAYERS, PARALLEL_CIRCLES, MERIDIAN_TOTAL), jnp.float32, -1.0, 1.0) * shard_levels(splits[3], (VERTICAL_LAYERS, PARALLEL_CIRCLES, MERIDIAN_TOTAL), ((1, 8), (2, 4)), -0.4, 0.0), -1.0, 1.0),
        "kinetic_coefficient": jnp.clip(jnp.exp(jax.random.uniform(splits[4], (REAC,), jnp.float32, math.log(0.05), math.log(1.0))), 0.05, 1.0),
        "thermal_exponent": jnp.clip(jax.random.uniform(splits[5], (REAC,), jnp.float32, -1.0, 1.0), -1.0, 1.0),
        "product_amounts": jnp.clip(jax.random.uniform(splits[6], (REAC, SPEC), jnp.float32, 0.0, 0.04), 0.0, 0.04),
        "reagent_pairs": place_ends(jax.random.randint(splits[7], (2, REAC), 0, SPEC), jax.random.fold_in(splits[7], 1), 0, SPEC - 1).astype(jnp.int32),
        "inner_iterations": draw_inner_iterations(jax.random.fold_in(splits[10], 71), 0),
        "smoothed_parallel_flags": draw_smoothed_parallel_flags(jax.random.fold_in(splits[10], 71), 0),
    }


chem_step = 1.0
polar_cut = 0.5
highest = lax.Precision.HIGHEST


def selection(reagent_pairs, species):
    indices = jnp.concatenate([reagent_pairs[0], reagent_pairs[1]])
    return (jnp.arange(species)[:, None] == indices[None, :]).astype(jnp.float32)


def substep(start_conc, warmth_degree, step_len, kinetic_coefficient, thermal_exponent, select, product_amounts):
    rate_coef = kinetic_coefficient[None, :] * jnp.exp(warmth_degree[:, None] * thermal_exponent[None, :])
    reactions = kinetic_coefficient.shape[0]
    amounts = start_conc
    for sweep in range(ITERS):
        reactant_conc = jnp.dot(amounts, select, precision=highest)
        first_conc = reactant_conc[:, :reactions]
        second = reactant_conc[:, reactions:]
        produced = jnp.dot(rate_coef * first_conc * second, product_amounts, precision=highest)
        loss_rate = jnp.dot(jnp.concatenate([rate_coef * second, rate_coef * first_conc], 1), select.T, precision=highest)
        amounts = (start_conc + step_len * produced) / (1.0 + step_len * loss_rate)
    return amounts


def minmod(left_val, right_val):
    return jnp.maximum(0.0, jnp.minimum(left_val, right_val)) + jnp.minimum(0.0, jnp.maximum(left_val, right_val))


def face_flux(padded, courant, axis_dim):
    extent = padded.shape[axis_dim]
    lower_cells = lax.slice_in_dim(padded, 0, extent - 2, axis=axis_dim)
    middle = lax.slice_in_dim(padded, 1, extent - 1, axis=axis_dim)
    upper_cells = lax.slice_in_dim(padded, 2, extent, axis=axis_dim)
    slopes = minmod(middle - lower_cells, upper_cells - middle)
    inner = extent - 2
    left_val = lax.slice_in_dim(middle, 0, inner - 1, axis=axis_dim)
    right_val = lax.slice_in_dim(middle, 1, inner, axis=axis_dim)
    left_slope = lax.slice_in_dim(slopes, 0, inner - 1, axis=axis_dim)
    right_slope = lax.slice_in_dim(slopes, 1, inner, axis=axis_dim)
    return jnp.where(courant >= 0.0, courant * (left_val + 0.5 * (1.0 - courant) * left_slope),
                     courant * (right_val - 0.5 * (1.0 + courant) * right_slope))


def reference(species_density, zonal_wall_ratio, meridional_wall_ratio, normalized_warmth, kinetic_coefficient, thermal_exponent, product_amounts, reagent_pairs, inner_iterations, smoothed_parallel_flags):
    select = selection(reagent_pairs, SPEC)
    grid_groupings = jnp.transpose(species_density.reshape(SPEC, VERTICAL_LAYERS, PARALLEL_CIRCLES, N_LON, MERIDIAN_PORTION), (1, 2, 3, 4, 0)).reshape(-1, MERIDIAN_PORTION, SPEC)
    warmer_groupings = normalized_warmth.reshape(-1, MERIDIAN_PORTION)
    repeats = inner_iterations.reshape(-1)

    def react_block(item):
        block, warmth_degree, repeat_count = item
        step_len = chem_step / repeat_count.astype(jnp.float32)

        def advance_once(index, amounts):
            return substep(amounts, warmth_degree, step_len, kinetic_coefficient, thermal_exponent, select, product_amounts)

        return lax.fori_loop(0, repeat_count, advance_once, block)

    reacted = lax.map(react_block, (grid_groupings, warmer_groupings, repeats))
    reacted = jnp.transpose(reacted.reshape(VERTICAL_LAYERS, PARALLEL_CIRCLES, N_LON, MERIDIAN_PORTION, SPEC), (4, 0, 1, 2, 3)).reshape(SPEC, VERTICAL_LAYERS, PARALLEL_CIRCLES, MERIDIAN_TOTAL)

    east_faces = jnp.concatenate([zonal_wall_ratio[:, :, -1:], zonal_wall_ratio], 2)
    north_faces = jnp.concatenate([jnp.zeros((VERTICAL_LAYERS, 1, MERIDIAN_TOTAL), jnp.float32), meridional_wall_ratio], 1)
    face_rows = jnp.arange(PARALLEL_CIRCLES + 1).astype(jnp.float32) * (math.pi / PARALLEL_CIRCLES) - math.pi / 2
    cell_rows = (jnp.arange(PARALLEL_CIRCLES).astype(jnp.float32) + 0.5) * (math.pi / PARALLEL_CIRCLES) - math.pi / 2
    face_weight = jnp.cos(face_rows)[:, None]
    cell_weight = jnp.cos(cell_rows)[:, None]
    ratio = jnp.cos(cell_rows) / polar_cut
    modes = jnp.arange(1, MERIDIAN_TOTAL // 2 + 1).astype(jnp.float32)
    keep = jnp.minimum(1.0, ratio[:, None] / jnp.sin(modes[None, :] * (math.pi / MERIDIAN_TOTAL)))
    damping = smoothed_parallel_flags.astype(jnp.float32)[:, None] * (1.0 - keep)
    damping = jnp.concatenate([jnp.zeros((PARALLEL_CIRCLES, 1), jnp.float32), damping], 1)

    def column(field):
        padded_lon = jnp.pad(field, ((0, 0), (0, 0), (2, 2)), mode="wrap")
        padded_lat = jnp.pad(field, ((0, 0), (2, 2), (0, 0)))
        east_flux = face_flux(padded_lon, east_faces, 2)
        north_flux = face_flux(padded_lat, north_faces, 1)
        weighted = face_weight * north_flux
        advected = field - (east_flux[:, :, 1:] - east_flux[:, :, :-1]) - (weighted[:, 1:, :] - weighted[:, :-1, :]) / cell_weight
        spectrum = jnp.fft.rfft(advected, axis=-1)
        return advected - jnp.fft.irfft(spectrum * damping, n=MERIDIAN_TOTAL, axis=-1)

    return lax.map(column, reacted)
```

```python
import math

import jax
import jax.numpy as jnp
from jax import lax
from jax.experimental import pallas as pl
from jax.experimental.pallas import tpu as pltpu
from jax.sharding import PartitionSpec as P

ITERS = 2
chunk = 256


chem_step = 1.0
polar_cut = 0.5
mode_block = 64
highest = lax.Precision.HIGHEST


def with_halo(block, sides, width, periodic):
    for axis, dim in sides:
        count = lax.axis_size(axis)
        forward = [(i, i + 1) for i in range(count - 1)]
        if periodic:
            forward.append((count - 1, 0))
        backward = [(target, source) for source, target in forward]
        low = lax.ppermute(
            lax.slice_in_dim(block, block.shape[dim] - width, None, axis=dim), axis, forward
        )
        high = lax.ppermute(lax.slice_in_dim(block, 0, width, axis=dim), axis, backward)
        block = jnp.concatenate([low, block, high], axis=dim)
    return block


def split(value):
    high = value.astype(jnp.bfloat16)
    low = (value - high.astype(jnp.float32)).astype(jnp.bfloat16)
    return high, low


def times(left_val, right_val):
    return jnp.dot(left_val, right_val, preferred_element_type=jnp.float32)


def chem_kernel(
    count_ref, conc_ref, warm_ref, kinetic_ref, thermal_ref, product_ref, pair_ref, out_ref,
    gather_ref, scatter_ref, product_t, rate_ref, state_ref
):
    lat_rows, species, cells = out_ref.shape
    reac = pair_ref.shape[1]
    sub = lax.broadcasted_iota(jnp.int32, (species, reac), 0)
    for side in range(2):
        chosen = jnp.where(sub == pair_ref[side : side + 1, :], 1.0, 0.0).astype(jnp.float32)
        flipped = chosen.T.astype(jnp.bfloat16)
        rows = pl.ds(side * reac, reac)
        gather_ref[rows, :] = jnp.concatenate([flipped, flipped], 1)
        scatter_ref[:, rows] = chosen.astype(jnp.bfloat16)
    high, low = split(product_ref[...].T)
    product_t[:species, :] = high
    product_t[species:, :] = low
    kinetic = jnp.broadcast_to(kinetic_ref[...], (cells, reac)).T
    thermal = jnp.broadcast_to(thermal_ref[...], (cells, reac)).T
    for row in range(lat_rows):
        rate_ref[:, pl.ds(row * cells, cells)] = kinetic * jnp.exp(
            thermal * warm_ref[row : row + 1, :]
        )
    lane = lax.broadcasted_iota(jnp.int32, (1, 2 * cells), 1)
    for pair in range(lat_rows // 2):
        first_row = 2 * pair
        state_ref[...] = jnp.concatenate(
            [conc_ref[pl.ds(first_row + i, species, stride=lat_rows), :] for i in range(2)], 1
        )
        counts = jnp.where(lane < cells, count_ref[first_row], count_ref[first_row + 1])
        step_len = chem_step / counts.astype(jnp.float32)
        columns = pl.ds(first_row * cells, 2 * cells)

        def advance_once(index, carry, counts=counts, step_len=step_len, columns=columns):
            start_conc = state_ref[...]
            amounts = start_conc
            for sweep in range(ITERS):
                stacked = jnp.concatenate(split(amounts), 0)
                produced = jnp.zeros_like(start_conc)
                loss_rate = jnp.zeros_like(start_conc)
                for part in range(0, reac, chunk):
                    rate_coef = rate_ref[pl.ds(part, chunk), columns]
                    first_conc = times(gather_ref[pl.ds(part, chunk), :], stacked)
                    second = times(gather_ref[pl.ds(reac + part, chunk), :], stacked)
                    rate_first = rate_coef * first_conc
                    made_high, made_low = split(rate_first * second)
                    both = times(product_t[:, pl.ds(part, chunk)], made_high)
                    produced += both[:species] + both[species:]
                    produced += times(product_t[:species, pl.ds(part, chunk)], made_low)
                    for start, value in ((part, rate_coef * second), (reac + part, rate_first)):
                        for piece in split(value):
                            loss_rate += times(scatter_ref[:, pl.ds(start, chunk)], piece)
                amounts = (start_conc + step_len * produced) / (1.0 + step_len * loss_rate)
            state_ref[...] = jnp.where(counts > index, amounts, start_conc)
            return carry

        turns = jnp.maximum(count_ref[first_row], count_ref[first_row + 1])
        lax.fori_loop(0, turns, advance_once, 0)
        for i in range(2):
            out_ref[first_row + i] = state_ref[:, i * cells : (i + 1) * cells]


def react(conc, warm, kinetic, thermal, product, pairs, counts):
    species = product.shape[1]
    reac = product.shape[0]
    lat_rows, cells = warm.shape
    vmem = pl.BlockSpec(memory_space=pltpu.VMEM)
    return pl.pallas_call(
        chem_kernel,
        out_shape=jax.ShapeDtypeStruct((lat_rows, species, cells), jnp.float32),
        in_specs=[pl.BlockSpec(memory_space=pltpu.SMEM)] + [vmem] * 6,
        out_specs=vmem,
        scratch_shapes=[
            pltpu.VMEM((2 * reac, 2 * species), jnp.bfloat16),
            pltpu.VMEM((species, 2 * reac), jnp.bfloat16),
            pltpu.VMEM((2 * species, reac), jnp.bfloat16),
            pltpu.VMEM((reac, lat_rows * cells), jnp.float32),
            pltpu.VMEM((species, 2 * cells), jnp.float32),
        ],
        compiler_params=pltpu.CompilerParams(vmem_limit_bytes=24 * 1024 * 1024),
    )(counts, conc, warm, kinetic, thermal, product, pairs)


def minmod(left_val, right_val):
    return jnp.maximum(0.0, jnp.minimum(left_val, right_val)) + jnp.minimum(
        0.0, jnp.maximum(left_val, right_val)
    )


def face_flux(padded, courant, axis_dim):
    extent = padded.shape[axis_dim]
    lower_cells = lax.slice_in_dim(padded, 0, extent - 2, axis=axis_dim)
    middle = lax.slice_in_dim(padded, 1, extent - 1, axis=axis_dim)
    upper_cells = lax.slice_in_dim(padded, 2, extent, axis=axis_dim)
    slopes = minmod(middle - lower_cells, upper_cells - middle)
    inner = extent - 2
    left_val = lax.slice_in_dim(middle, 0, inner - 1, axis=axis_dim)
    right_val = lax.slice_in_dim(middle, 1, inner, axis=axis_dim)
    left_slope = lax.slice_in_dim(slopes, 0, inner - 1, axis=axis_dim)
    right_slope = lax.slice_in_dim(slopes, 1, inner, axis=axis_dim)
    return jnp.where(
        courant >= 0.0,
        courant * (left_val + 0.5 * (1.0 - courant) * left_slope),
        courant * (right_val - 0.5 * (1.0 + courant) * right_slope),
    )


def remove_modes(lines_in, factor, lat_rows, total_lon):
    held = lines_in.shape[0]
    signal = lines_in.reshape(held * lat_rows, total_lon)
    scales = jnp.tile(factor, (held, 1))
    positions = jnp.arange(total_lon)[:, None]
    half_modes = total_lon // 2

    def mode_turn(turn, removed):
        first_mode = turn * mode_block
        phase = positions * (first_mode + 1 + jnp.arange(mode_block))[None, :] % total_lon
        angle = phase.astype(jnp.float32) * (2.0 * math.pi / total_lon)
        table = jnp.concatenate([jnp.cos(angle), jnp.sin(angle)], 1)
        coeffs = jnp.dot(signal, table, precision=highest)
        scale_part = lax.dynamic_slice_in_dim(scales, first_mode, mode_block, 1)
        coeffs = coeffs * jnp.concatenate([scale_part, scale_part], 1)
        return removed + jnp.dot(coeffs, table.T, precision=highest)

    removed = lax.fori_loop(0, half_modes // mode_block, mode_turn, jnp.zeros_like(signal))
    return (signal - removed).reshape(lines_in.shape)


def per_device(
    species_density,
    zonal_wall_ratio,
    meridional_wall_ratio,
    normalized_warmth,
    kinetic_coefficient,
    thermal_exponent,
    product_amounts,
    reagent_pairs,
    inner_iterations,
    smoothed_parallel_flags,
):
    species, level_list, lat_rows, meridian_boxes = species_density.shape
    lat_devices = lax.axis_size("lat")
    lon_devices = lax.axis_size("lon")
    total_rows = lat_rows * lat_devices
    total_lon = meridian_boxes * lon_devices
    row_base = lax.axis_index("lat") * lat_rows
    reacted = react(
        species_density.reshape(species * lat_rows, meridian_boxes),
        normalized_warmth.reshape(lat_rows, meridian_boxes),
        kinetic_coefficient.reshape(1, -1),
        thermal_exponent.reshape(1, -1),
        product_amounts,
        reagent_pairs,
        inner_iterations.reshape(lat_rows),
    )
    reacted = jnp.transpose(reacted, (1, 0, 2))[:, None]
    fields = jnp.concatenate([reacted, zonal_wall_ratio[None], meridional_wall_ratio[None]], 0)
    along_lon = with_halo(fields, (("lon", 3),), 2, True)
    along_lat = with_halo(fields, (("lat", 2),), 2, False)
    east_flux = face_flux(along_lon[:species], along_lon[species, :, :, 1:-2], 3)
    north_flux = face_flux(along_lat[:species], along_lat[species + 1, :, 1:-2, :], 2)
    face_rows = (row_base + jnp.arange(lat_rows + 1)).astype(jnp.float32) * (
        math.pi / total_rows
    ) - math.pi / 2
    cell_rows = ((row_base + jnp.arange(lat_rows)).astype(jnp.float32) + 0.5) * (
        math.pi / total_rows
    ) - math.pi / 2
    face_weight = jnp.cos(face_rows)[:, None]
    cell_weight = jnp.cos(cell_rows)[:, None]
    weighted = face_weight * north_flux
    advected = (
        reacted
        - (east_flux[..., 1:] - east_flux[..., :-1])
        - (weighted[:, :, 1:, :] - weighted[:, :, :-1, :]) / cell_weight
    )
    half_modes = total_lon // 2
    ratio = jnp.cos(cell_rows) / polar_cut
    modes = jnp.arange(1, half_modes + 1).astype(jnp.float32)
    keep = jnp.minimum(1.0, ratio[:, None] / jnp.sin(modes[None, :] * (math.pi / total_lon)))
    mode_weight = jnp.where(jnp.arange(1, half_modes + 1) == half_modes, 1.0, 2.0)
    factor = (
        smoothed_parallel_flags.astype(jnp.float32)[:, None]
        * (1.0 - keep)
        * mode_weight[None, :]
        / total_lon
    )
    lines = advected.reshape(
        species * level_list // lon_devices, lon_devices, lat_rows, meridian_boxes
    )
    smoothed = remove_modes(
        lax.all_to_all(lines, "lon", split_axis=1, concat_axis=3, tiled=True),
        factor,
        lat_rows,
        total_lon,
    )
    filtered = lax.all_to_all(smoothed, "lon", split_axis=3, concat_axis=1, tiled=True)
    return filtered.reshape(species, level_list, lat_rows, meridian_boxes)


def solution(mesh):
    placed = (
        P(None, None, "lat", "lon"),
        P(None, "lat", "lon"),
        P(None, "lat", "lon"),
        P(None, "lat", "lon"),
        P(),
        P(),
        P(),
        P(),
        P(None, "lat", "lon"),
        P("lat"),
    )
    return jax.shard_map(
        per_device,
        mesh=mesh,
        in_specs=placed,
        out_specs=P(None, None, "lat", "lon"),
        check_vma=False,
    )
```

```python
import functools
import math

import jax
import jax.numpy as jnp
import numpy as np
from jax import lax
from jax.experimental import pallas as pl
from jax.experimental.pallas import tpu as pltpu
from jax.sharding import PartitionSpec as P

ITERS = 2
chunk = 256


chem_step = 1.0
polar_cut = 0.5


def split(value):
    high = value.astype(jnp.bfloat16)
    low = (value - high.astype(jnp.float32)).astype(jnp.bfloat16)
    return high, low


def times(left_val, right_val):
    return jnp.dot(left_val, right_val, preferred_element_type=jnp.float32)


def chem_kernel(
    count_ref, conc_ref, warm_ref, kinetic_ref, thermal_ref, product_ref, pair_ref, out_ref,
    gather_ref, scatter_ref, product_t, rate_ref, state_ref
):
    lat_rows, species, cells = out_ref.shape
    reac = pair_ref.shape[1]
    sub = lax.broadcasted_iota(jnp.int32, (species, reac), 0)
    for side in range(2):
        chosen = jnp.where(sub == pair_ref[side : side + 1, :], 1.0, 0.0).astype(jnp.float32)
        flipped = chosen.T.astype(jnp.bfloat16)
        rows = pl.ds(side * reac, reac)
        gather_ref[rows, :] = jnp.concatenate([flipped, flipped], 1)
        scatter_ref[:, rows] = chosen.astype(jnp.bfloat16)
    high, low = split(product_ref[...].T)
    product_t[:species, :] = high
    product_t[species:, :] = low
    kinetic = jnp.broadcast_to(kinetic_ref[...], (cells, reac)).T
    thermal = jnp.broadcast_to(thermal_ref[...], (cells, reac)).T
    for row in range(lat_rows):
        rate_ref[:, pl.ds(row * cells, cells)] = kinetic * jnp.exp(
            thermal * warm_ref[row : row + 1, :]
        )
    lane = lax.broadcasted_iota(jnp.int32, (1, 2 * cells), 1)
    for pair in range(lat_rows // 2):
        first_row = 2 * pair
        state_ref[...] = jnp.concatenate(
            [conc_ref[pl.ds(first_row + i, species, stride=lat_rows), :] for i in range(2)], 1
        )
        counts = jnp.where(lane < cells, count_ref[first_row], count_ref[first_row + 1])
        step_len = chem_step / counts.astype(jnp.float32)
        columns = pl.ds(first_row * cells, 2 * cells)

        def advance_once(index, carry, counts=counts, step_len=step_len, columns=columns):
            start_conc = state_ref[...]
            amounts = start_conc
            for sweep in range(ITERS):
                stacked = jnp.concatenate(split(amounts), 0)
                produced = jnp.zeros_like(start_conc)
                loss_rate = jnp.zeros_like(start_conc)
                for part in range(0, reac, chunk):
                    rate_coef = rate_ref[pl.ds(part, chunk), columns]
                    first_conc = times(gather_ref[pl.ds(part, chunk), :], stacked)
                    second = times(gather_ref[pl.ds(reac + part, chunk), :], stacked)
                    rate_first = rate_coef * first_conc
                    made_high, made_low = split(rate_first * second)
                    both = times(product_t[:, pl.ds(part, chunk)], made_high)
                    produced += both[:species] + both[species:]
                    produced += times(product_t[:species, pl.ds(part, chunk)], made_low)
                    for start, value in ((part, rate_coef * second), (reac + part, rate_first)):
                        for piece in split(value):
                            loss_rate += times(scatter_ref[:, pl.ds(start, chunk)], piece)
                amounts = (start_conc + step_len * produced) / (1.0 + step_len * loss_rate)
            state_ref[...] = jnp.where(counts > index, amounts, start_conc)
            return carry

        turns = jnp.maximum(count_ref[first_row], count_ref[first_row + 1])
        lax.fori_loop(0, turns, advance_once, 0)
        for i in range(2):
            out_ref[first_row + i] = state_ref[:, i * cells : (i + 1) * cells]


def react(conc, warm, kinetic, thermal, product, pairs, counts):
    species = product.shape[1]
    reac = product.shape[0]
    lat_rows, cells = warm.shape
    vmem = pl.BlockSpec(memory_space=pltpu.VMEM)
    return pl.pallas_call(
        chem_kernel,
        out_shape=jax.ShapeDtypeStruct((lat_rows, species, cells), jnp.float32),
        in_specs=[pl.BlockSpec(memory_space=pltpu.SMEM)] + [vmem] * 6,
        out_specs=vmem,
        scratch_shapes=[
            pltpu.VMEM((2 * reac, 2 * species), jnp.bfloat16),
            pltpu.VMEM((species, 2 * reac), jnp.bfloat16),
            pltpu.VMEM((2 * species, reac), jnp.bfloat16),
            pltpu.VMEM((reac, lat_rows * cells), jnp.float32),
            pltpu.VMEM((species, 2 * cells), jnp.float32),
        ],
        compiler_params=pltpu.CompilerParams(vmem_limit_bytes=24 * 1024 * 1024),
    )(counts, conc, warm, kinetic, thermal, product, pairs)


def minmod(left_val, right_val):
    return jnp.maximum(0.0, jnp.minimum(left_val, right_val)) + jnp.minimum(
        0.0, jnp.maximum(left_val, right_val)
    )


MESH = pl.DeviceIdType.MESH


def row_tables(total_rows, total_lon):
    faces = np.arange(total_rows + 1) * (math.pi / total_rows) - math.pi / 2
    centres = (np.arange(total_rows) + 0.5) * (math.pi / total_rows) - math.pi / 2
    modes = np.arange(1, total_lon // 2 + 1)
    ratio = np.cos(centres) / polar_cut
    keep = np.minimum(1.0, ratio[:, None] / np.sin(modes[None, :] * (math.pi / total_lon)))
    damp = np.concatenate([np.zeros((total_rows, 1)), 1.0 - keep], 1)
    taps = np.fft.irfft(damp, n=total_lon, axis=1)
    weights = np.zeros((total_rows, 128))
    weights[:, 0] = np.cos(faces[1:]) / np.cos(centres)
    weights[:, 1] = np.cos(faces[:-1]) / np.cos(centres)
    return np.concatenate([taps, weights], 1).astype(np.float32)


def upwind(courant):
    plus = jnp.maximum(courant, 0.0)
    minus = jnp.minimum(courant, 0.0)
    return plus, 0.5 * plus * (1.0 - courant), minus, 0.5 * minus * (1.0 + courant)


def flux(parts, low, low_slope, high, high_slope):
    plus, plus_slope, minus, minus_slope = parts
    return (plus * low + plus_slope * low_slope) + (minus * high - minus_slope * high_slope)


def transport_kernel(
    lats, lons, react_ref, zonal_ref, meridional_ref, table_ref, flag_ref, out_ref,
    edge_ref, edge_in, lat_in, meridional_in, moved_ref, circle_ref, result_ref, back_ref,
    edge_send, edge_recv, lat_send, lat_recv, wall_send, wall_recv,
    to_send, to_recv, from_send, from_recv
):
    rows, species, cells = react_ref.shape
    share = species // lons
    total_lon = lons * cells
    lat = lax.axis_index("lat")
    lon = lax.axis_index("lon")
    has_north = lat < lats - 1
    has_south = lat > 0
    quarter = lats // 4
    polar = jnp.logical_or(lat < quarter, lat >= lats - quarter)

    barrier = pltpu.get_barrier_semaphore()
    for step in range(1, lons):
        pl.semaphore_signal(
            barrier, inc=1, device_id=(lat, lax.rem(lon + step, lons)), device_id_type=MESH
        )

    @pl.when(has_north)
    def _():
        pl.semaphore_signal(barrier, inc=1, device_id=(lat + 1, lon), device_id_type=MESH)

    @pl.when(has_south)
    def _():
        pl.semaphore_signal(barrier, inc=1, device_id=(lat - 1, lon), device_id_type=MESH)

    for row in range(rows):
        turned = react_ref[row].T
        edge_ref[0, row] = turned[cells - 8 :]
        edge_ref[1, row] = turned[:8]
    edge_ref[0, rows, :rows] = zonal_ref[...]
    edge_ref[1, rows, :rows] = zonal_ref[...]

    @pl.when(jnp.logical_not(has_south))
    def _():
        lat_in[0] = jnp.zeros((2, species, cells), jnp.float32)
        meridional_in[...] = jnp.zeros((rows, cells), jnp.float32)

    @pl.when(jnp.logical_not(has_north))
    def _():
        lat_in[1] = jnp.zeros((2, species, cells), jnp.float32)

    neighbours = lons - 1 + has_north.astype(jnp.int32) + has_south.astype(jnp.int32)
    pl.semaphore_wait(barrier, neighbours)

    def edge_copy(side):
        target = lax.rem(lon + 1, lons) if side == 0 else lax.rem(lon + lons - 1, lons)
        return pltpu.make_async_remote_copy(
            src_ref=edge_ref.at[side], dst_ref=edge_in.at[side],
            send_sem=edge_send.at[side], recv_sem=edge_recv.at[side],
            device_id=(lat, target), device_id_type=MESH,
        )

    def lat_copy(side):
        first = rows - 2 if side == 0 else 0
        return pltpu.make_async_remote_copy(
            src_ref=react_ref.at[pl.ds(first, 2)], dst_ref=lat_in.at[side],
            send_sem=lat_send.at[side], recv_sem=lat_recv.at[side],
            device_id=(lat + 1 if side == 0 else lat - 1, lon), device_id_type=MESH,
        )

    wall_copy = pltpu.make_async_remote_copy(
        src_ref=meridional_ref, dst_ref=meridional_in,
        send_sem=wall_send, recv_sem=wall_recv,
        device_id=(lat + 1, lon), device_id_type=MESH,
    )
    edge_copies = [edge_copy(0), edge_copy(1)]
    lat_copies = [lat_copy(0), lat_copy(1)]
    for copy in edge_copies:
        copy.start()

    @pl.when(has_north)
    def _():
        lat_copies[0].start()
        wall_copy.start()

    @pl.when(has_south)
    def _():
        lat_copies[1].start()

    for copy in edge_copies:
        copy.wait_recv()

    lane = lax.broadcasted_iota(jnp.int32, (1, cells), 1)
    gap = jnp.zeros((cells - 16, species), jnp.float32)
    for row in range(rows):
        here = react_ref[row]
        outside = jnp.concatenate([edge_in[1, row], gap, edge_in[0, row]], 0).T
        west = pltpu.roll(jnp.where(lane == cells - 1, outside, here), 1, 1)
        west_two = pltpu.roll(jnp.where(lane >= cells - 2, outside, here), 2, 1)
        east = pltpu.roll(jnp.where(lane == 0, outside, here), cells - 1, 1)
        east_two = pltpu.roll(jnp.where(lane < 2, outside, here), cells - 2, 1)
        west_step = here - west
        east_step = east - here
        slope = minmod(west_step, east_step)
        west_slope = minmod(west - west_two, west_step)
        east_slope = minmod(east_step, east_two - east)
        courant = zonal_ref[row : row + 1, :]
        courant_west = pltpu.roll(
            jnp.where(lane == cells - 1, edge_in[0, rows, row : row + 1, :], courant), 1, 1
        )
        leaving = flux(upwind(courant), here, slope, east, east_slope)
        entering = flux(upwind(courant_west), west, west_slope, here, slope)
        moved_ref[row] = here - (leaving - entering)

    @pl.when(has_south)
    def _():
        lat_copies[0].wait_recv()
        wall_copy.wait_recv()

    @pl.when(has_north)
    def _():
        lat_copies[1].wait_recv()

    def line(row):
        if row < 0:
            return lat_in[0, row + 2]
        if row >= rows:
            return lat_in[1, row - rows]
        return react_ref[row]

    def circle_copy(row, step):
        target = lax.rem(lon + step, lons)
        return pltpu.make_async_remote_copy(
            src_ref=moved_ref.at[row, pl.ds(pl.multiple_of(target * share, share), share)],
            dst_ref=circle_ref.at[row, lon],
            send_sem=to_send.at[row, step], recv_sem=to_recv.at[row, step],
            device_id=(lat, target), device_id_type=MESH,
        )

    def back_copy(row, step):
        target = lax.rem(lon + step, lons)
        return pltpu.make_async_remote_copy(
            src_ref=result_ref.at[row, target],
            dst_ref=back_ref.at[row, pl.ds(pl.multiple_of(lon * share, share), share)],
            send_sem=from_send.at[row, step], recv_sem=from_recv.at[row, step],
            device_id=(lat, target), device_id_type=MESH,
        )

    own = pl.ds(pl.multiple_of(lon * share, share), share)
    south_flux = None
    step_below = line(-1) - line(-2)
    step_here = line(0) - line(-1)
    slope_low = minmod(step_below, step_here)
    for row in range(-1, rows):
        step_above = line(row + 2) - line(row + 1)
        slope_high = minmod(step_here, step_above)
        courant = meridional_in[rows - 1 :, :] if row < 0 else meridional_ref[row : row + 1, :]
        north_flux = flux(upwind(courant), line(row), slope_low, line(row + 1), slope_high)
        if row >= 0:
            weights = table_ref[lat, row : row + 1, total_lon:]
            moved = moved_ref[row] - (
                weights[:, 0:1] * north_flux - weights[:, 1:2] * south_flux
            )
            moved_ref[row] = moved
            out_ref[pl.ds(row, species, stride=rows), :] = moved

            @pl.when(polar)
            def _(row=row):
                for step in range(1, lons):
                    circle_copy(row, step).start()
                circle_ref[row, lon] = moved_ref[row, own]

        south_flux = north_flux
        slope_low = slope_high
        step_here = step_above

    @pl.when(polar)
    def _():
        for row in range(rows):
            taps = table_ref[lat, row : row + 1, :total_lon]
            taps = taps * flag_ref[row].astype(jnp.float32)
            spread = pltpu.roll(
                jnp.broadcast_to(taps, (cells, total_lon)), 0, 1, stride=1, stride_axis=0
            )
            spread_high, spread_low = split(spread)
            for step in range(1, lons):
                circle_copy(row, step).wait_recv()
            signal = circle_ref[row].reshape(species, cells)
            high, low = split(signal)
            product = (
                times(high, spread_high) + times(low, spread_high) + times(high, spread_low)
            )
            for target in range(lons):
                value = signal[target * share : (target + 1) * share]
                for source in range(lons):
                    offset = (target - source) % lons * cells
                    value -= product[
                        source * share : (source + 1) * share, offset : offset + cells
                    ]
                result_ref[row, target] = value
            for step in range(1, lons):
                back_copy(row, step).start()
            back_ref[row, own] = result_ref[row, lon]
        for row in range(rows):
            for step in range(1, lons):
                back_copy(row, step).wait_recv()
            out_ref[pl.ds(row, species, stride=rows), :] = back_ref[row]
        for row in range(rows):
            for step in range(1, lons):
                circle_copy(row, step).wait_send()
                back_copy(row, step).wait_send()

    for copy in edge_copies:
        copy.wait_send()

    @pl.when(has_north)
    def _():
        lat_copies[0].wait_send()
        wall_copy.wait_send()

    @pl.when(has_south)
    def _():
        lat_copies[1].wait_send()


def transport(lats, lons, reacted, zonal, meridional, table, flags):
    rows, species, cells = reacted.shape
    share = species // lons
    vmem = pl.BlockSpec(memory_space=pltpu.VMEM)
    real = jnp.float32
    dma = pltpu.SemaphoreType.DMA
    return pl.pallas_call(
        functools.partial(transport_kernel, lats, lons),
        out_shape=jax.ShapeDtypeStruct((rows * species, cells), real),
        in_specs=[vmem] * 4 + [pl.BlockSpec(memory_space=pltpu.SMEM)],
        out_specs=vmem,
        scratch_shapes=[
            pltpu.VMEM((2, rows + 1, 8, cells), real),
            pltpu.VMEM((2, rows + 1, 8, cells), real),
            pltpu.VMEM((2, 2, species, cells), real),
            pltpu.VMEM((rows, cells), real),
            pltpu.VMEM((rows, species, cells), real),
            pltpu.VMEM((rows, lons, share, cells), real),
            pltpu.VMEM((rows, lons, share, cells), real),
            pltpu.VMEM((rows, species, cells), real),
            dma((2,)), dma((2,)), dma((2,)), dma((2,)), dma, dma,
            dma((rows, lons)), dma((rows, lons)), dma((rows, lons)), dma((rows, lons)),
        ],
        compiler_params=pltpu.CompilerParams(
            collective_id=0, has_side_effects=True, vmem_limit_bytes=24 * 1024 * 1024
        ),
    )(reacted, zonal, meridional, table, flags)


def per_device(
    species_density,
    zonal_wall_ratio,
    meridional_wall_ratio,
    normalized_warmth,
    kinetic_coefficient,
    thermal_exponent,
    product_amounts,
    reagent_pairs,
    inner_iterations,
    smoothed_parallel_flags,
):
    species, level_list, lat_rows, meridian_boxes = species_density.shape
    lat_devices = lax.axis_size("lat")
    lon_devices = lax.axis_size("lon")
    reacted = react(
        species_density.reshape(species * lat_rows, meridian_boxes),
        normalized_warmth.reshape(lat_rows, meridian_boxes),
        kinetic_coefficient.reshape(1, -1),
        thermal_exponent.reshape(1, -1),
        product_amounts,
        reagent_pairs,
        inner_iterations.reshape(lat_rows),
    )
    table = row_tables(lat_rows * lat_devices, meridian_boxes * lon_devices)
    filtered = transport(
        lat_devices,
        lon_devices,
        reacted,
        zonal_wall_ratio.reshape(lat_rows, meridian_boxes),
        meridional_wall_ratio.reshape(lat_rows, meridian_boxes),
        jnp.asarray(table).reshape(lat_devices, lat_rows, -1),
        smoothed_parallel_flags,
    )
    return filtered.reshape(species, level_list, lat_rows, meridian_boxes)


def solution(mesh):
    placed = (
        P(None, None, "lat", "lon"),
        P(None, "lat", "lon"),
        P(None, "lat", "lon"),
        P(None, "lat", "lon"),
        P(),
        P(),
        P(),
        P(),
        P(None, "lat", "lon"),
        P("lat"),
    )
    return jax.shard_map(
        per_device,
        mesh=mesh,
        in_specs=placed,
        out_specs=P(None, None, "lat", "lon"),
        check_vma=False,
    )
```

```python
import functools
import math

import jax
import jax.numpy as jnp
import numpy as np
from jax import lax
from jax.experimental import pallas as pl
from jax.experimental.pallas import tpu as pltpu
from jax.sharding import PartitionSpec as P

ITERS = 2
chunk = 256
group = 2
chem_vmem = 56 * 1024 * 1024


chem_step = 1.0
polar_cut = 0.5


def split(value):
    high = value.astype(jnp.bfloat16)
    low = (value - high.astype(jnp.float32)).astype(jnp.bfloat16)
    return high, low


def times(left_val, right_val):
    return jnp.dot(left_val, right_val, preferred_element_type=jnp.float32)


def chem_kernel(
    count_ref, conc_hbm, warm_hbm, kinetic_hbm, thermal_hbm, product_hbm, pair_hbm, out_ref,
    conc_ref, warm_ref, kinetic_ref, thermal_ref, product_ref, pair_ref,
    gather_ref, collect_ref, rate_ref, state_ref, sems
):
    lat_rows, species, cells = out_ref.shape
    reac = pair_ref.shape[1]
    loads = [
        pltpu.make_async_copy(source, target, sems.at[i])
        for i, (source, target) in enumerate(
            (
                (pair_hbm, pair_ref),
                (kinetic_hbm, kinetic_ref),
                (thermal_hbm, thermal_ref),
                (warm_hbm, warm_ref),
                (product_hbm, product_ref),
                (conc_hbm, conc_ref),
            )
        )
    ]
    for load in loads:
        load.start()
    loads[0].wait()
    sub = lax.broadcasted_iota(jnp.int32, (species, reac), 0)
    used = jnp.zeros((species, reac), jnp.float32)
    for side in range(2):
        chosen = jnp.where(sub == pair_ref[side : side + 1, :], 1.0, 0.0).astype(jnp.float32)
        flipped = chosen.T.astype(jnp.bfloat16)
        gather_ref[pl.ds(side * reac, reac), :] = jnp.concatenate([flipped, flipped], 1)
        used += chosen
    collect_ref[species : 2 * species, :] = used.astype(jnp.bfloat16)
    for load in loads[1:4]:
        load.wait()
    kinetic = jnp.broadcast_to(kinetic_ref[...], (cells, reac)).T
    thermal = jnp.broadcast_to(thermal_ref[...], (cells, reac)).T
    for row in range(lat_rows):
        rate_ref[:, pl.ds(row * cells, cells)] = kinetic * jnp.exp(
            thermal * warm_ref[row : row + 1, :]
        )
    loads[4].wait()
    high, low = split(product_ref[...].T)
    collect_ref[:species, :] = high
    collect_ref[2 * species :, :] = low
    loads[5].wait()
    owner = lax.broadcasted_iota(jnp.int32, (1, lat_rows * cells), 1) // cells
    counts_all = jnp.full((1, lat_rows * cells), count_ref[0], jnp.int32)
    for row in range(lat_rows):
        counts_all = jnp.where(owner == row, count_ref[row], counts_all)
        state_ref[:, row * cells : (row + 1) * cells] = conc_ref[
            pl.ds(row, species, stride=lat_rows), :
        ]

    def turns_of(first_row):
        turns = count_ref[first_row]
        for row in range(first_row + 1, first_row + group):
            turns = jnp.maximum(turns, count_ref[row])
        return turns

    def run(first_row, size, begin, end):
        columns = slice(first_row * cells, (first_row + size) * cells)
        counts = counts_all[:, columns]
        step_len = chem_step / counts.astype(jnp.float32)

        def advance_once(index, carry):
            start_conc = state_ref[:, columns]
            amounts = start_conc
            for sweep in range(ITERS):
                stacked = jnp.concatenate(split(amounts), 0)
                produced = jnp.zeros_like(start_conc)
                lost = jnp.zeros_like(start_conc)
                for part in range(0, reac, chunk):
                    reactions = pl.ds(part, chunk)
                    first_conc = times(gather_ref[reactions, :], stacked)
                    second = times(gather_ref[pl.ds(reac + part, chunk), :], stacked)
                    made = rate_ref[reactions, columns] * first_conc * second
                    made_high, made_low = split(made)
                    main = times(collect_ref[:, reactions], made_high)
                    rest = times(collect_ref[: 2 * species, reactions], made_low)
                    produced += main[:species] + (main[2 * species :] + rest[:species])
                    lost += main[species : 2 * species] + rest[species:]
                loss_rate = lost / amounts
                amounts = (start_conc + step_len * produced) / (1.0 + step_len * loss_rate)
            state_ref[:, columns] = jnp.where(counts > index, amounts, start_conc)
            return carry

        lax.fori_loop(begin, end, advance_once, 0)

    groups = range(0, lat_rows, group)
    together = turns_of(0)
    for first_row in groups:
        together = jnp.minimum(together, turns_of(first_row))
    run(0, lat_rows, 0, together)
    for first_row in groups:
        run(first_row, group, together, turns_of(first_row))
    for row in range(lat_rows):
        out_ref[row] = state_ref[:, row * cells : (row + 1) * cells]


def react(conc, warm, kinetic, thermal, product, pairs, counts):
    species = product.shape[1]
    reac = product.shape[0]
    lat_rows, cells = warm.shape
    operands = (conc, warm, kinetic, thermal, product, pairs)
    anywhere = pl.BlockSpec(memory_space=pl.ANY)
    return pl.pallas_call(
        chem_kernel,
        out_shape=jax.ShapeDtypeStruct((lat_rows, species, cells), jnp.float32),
        in_specs=[pl.BlockSpec(memory_space=pltpu.SMEM)] + [anywhere] * len(operands),
        out_specs=pl.BlockSpec(memory_space=pltpu.VMEM),
        scratch_shapes=[pltpu.VMEM(value.shape, value.dtype) for value in operands]
        + [
            pltpu.VMEM((2 * reac, 2 * species), jnp.bfloat16),
            pltpu.VMEM((3 * species, reac), jnp.bfloat16),
            pltpu.VMEM((reac, lat_rows * cells), jnp.float32),
            pltpu.VMEM((species, lat_rows * cells), jnp.float32),
            pltpu.SemaphoreType.DMA((len(operands),)),
        ],
        compiler_params=pltpu.CompilerParams(vmem_limit_bytes=chem_vmem),
    )(counts, *operands)


def minmod(left_val, right_val):
    return jnp.maximum(0.0, jnp.minimum(left_val, right_val)) + jnp.minimum(
        0.0, jnp.maximum(left_val, right_val)
    )


MESH = pl.DeviceIdType.MESH


def row_tables(total_rows, total_lon):
    faces = np.arange(total_rows + 1) * (math.pi / total_rows) - math.pi / 2
    centres = (np.arange(total_rows) + 0.5) * (math.pi / total_rows) - math.pi / 2
    modes = np.arange(1, total_lon // 2 + 1)
    ratio = np.cos(centres) / polar_cut
    keep = np.minimum(1.0, ratio[:, None] / np.sin(modes[None, :] * (math.pi / total_lon)))
    damp = np.concatenate([np.zeros((total_rows, 1)), 1.0 - keep], 1)
    taps = np.fft.irfft(damp, n=total_lon, axis=1)
    weights = np.zeros((total_rows, 128))
    weights[:, 0] = np.cos(faces[1:]) / np.cos(centres)
    weights[:, 1] = np.cos(faces[:-1]) / np.cos(centres)
    return np.concatenate([taps, weights], 1).astype(np.float32)


def upwind(courant):
    plus = jnp.maximum(courant, 0.0)
    minus = jnp.minimum(courant, 0.0)
    return plus, 0.5 * plus * (1.0 - courant), minus, 0.5 * minus * (1.0 + courant)


def flux(parts, low, low_slope, high, high_slope):
    plus, plus_slope, minus, minus_slope = parts
    return (plus * low + plus_slope * low_slope) + (minus * high - minus_slope * high_slope)


def transport_kernel(
    lats, lons, react_ref, zonal_ref, meridional_ref, table_ref, flag_ref, out_ref,
    edge_ref, edge_in, lat_in, meridional_in, moved_ref, circle_ref, result_ref, back_ref,
    edge_send, edge_recv, lat_send, lat_recv, wall_send, wall_recv,
    to_send, to_recv, from_send, from_recv
):
    rows, species, cells = react_ref.shape
    share = species // lons
    total_lon = lons * cells
    lat = lax.axis_index("lat")
    lon = lax.axis_index("lon")
    has_north = lat < lats - 1
    has_south = lat > 0
    quarter = lats // 4
    polar = jnp.logical_or(lat < quarter, lat >= lats - quarter)

    barrier = pltpu.get_barrier_semaphore()
    for step in range(1, lons):
        pl.semaphore_signal(
            barrier, inc=1, device_id=(lat, lax.rem(lon + step, lons)), device_id_type=MESH
        )

    @pl.when(has_north)
    def _():
        pl.semaphore_signal(barrier, inc=1, device_id=(lat + 1, lon), device_id_type=MESH)

    @pl.when(has_south)
    def _():
        pl.semaphore_signal(barrier, inc=1, device_id=(lat - 1, lon), device_id_type=MESH)

    for row in range(rows):
        turned = react_ref[row].T
        edge_ref[0, row] = turned[cells - 8 :]
        edge_ref[1, row] = turned[:8]
    edge_ref[0, rows, :rows] = zonal_ref[...]
    edge_ref[1, rows, :rows] = zonal_ref[...]

    @pl.when(jnp.logical_not(has_south))
    def _():
        lat_in[0] = jnp.zeros((2, species, cells), jnp.float32)
        meridional_in[...] = jnp.zeros((rows, cells), jnp.float32)

    @pl.when(jnp.logical_not(has_north))
    def _():
        lat_in[1] = jnp.zeros((2, species, cells), jnp.float32)

    neighbours = lons - 1 + has_north.astype(jnp.int32) + has_south.astype(jnp.int32)
    pl.semaphore_wait(barrier, neighbours)

    def edge_copy(side):
        target = lax.rem(lon + 1, lons) if side == 0 else lax.rem(lon + lons - 1, lons)
        return pltpu.make_async_remote_copy(
            src_ref=edge_ref.at[side], dst_ref=edge_in.at[side],
            send_sem=edge_send.at[side], recv_sem=edge_recv.at[side],
            device_id=(lat, target), device_id_type=MESH,
        )

    def lat_copy(side):
        first = rows - 2 if side == 0 else 0
        return pltpu.make_async_remote_copy(
            src_ref=react_ref.at[pl.ds(first, 2)], dst_ref=lat_in.at[side],
            send_sem=lat_send.at[side], recv_sem=lat_recv.at[side],
            device_id=(lat + 1 if side == 0 else lat - 1, lon), device_id_type=MESH,
        )

    wall_copy = pltpu.make_async_remote_copy(
        src_ref=meridional_ref, dst_ref=meridional_in,
        send_sem=wall_send, recv_sem=wall_recv,
        device_id=(lat + 1, lon), device_id_type=MESH,
    )
    edge_copies = [edge_copy(0), edge_copy(1)]
    lat_copies = [lat_copy(0), lat_copy(1)]
    for copy in edge_copies:
        copy.start()

    @pl.when(has_north)
    def _():
        lat_copies[0].start()
        wall_copy.start()

    @pl.when(has_south)
    def _():
        lat_copies[1].start()

    for copy in edge_copies:
        copy.wait_recv()

    lane = lax.broadcasted_iota(jnp.int32, (1, cells), 1)
    gap = jnp.zeros((cells - 16, species), jnp.float32)
    for row in range(rows):
        here = react_ref[row]
        outside = jnp.concatenate([edge_in[1, row], gap, edge_in[0, row]], 0).T
        west = pltpu.roll(jnp.where(lane == cells - 1, outside, here), 1, 1)
        west_two = pltpu.roll(jnp.where(lane >= cells - 2, outside, here), 2, 1)
        east = pltpu.roll(jnp.where(lane == 0, outside, here), cells - 1, 1)
        east_two = pltpu.roll(jnp.where(lane < 2, outside, here), cells - 2, 1)
        west_step = here - west
        east_step = east - here
        slope = minmod(west_step, east_step)
        west_slope = minmod(west - west_two, west_step)
        east_slope = minmod(east_step, east_two - east)
        courant = zonal_ref[row : row + 1, :]
        courant_west = pltpu.roll(
            jnp.where(lane == cells - 1, edge_in[0, rows, row : row + 1, :], courant), 1, 1
        )
        leaving = flux(upwind(courant), here, slope, east, east_slope)
        entering = flux(upwind(courant_west), west, west_slope, here, slope)
        moved_ref[row] = here - (leaving - entering)

    @pl.when(has_south)
    def _():
        lat_copies[0].wait_recv()
        wall_copy.wait_recv()

    @pl.when(has_north)
    def _():
        lat_copies[1].wait_recv()

    def line(row):
        if row < 0:
            return lat_in[0, row + 2]
        if row >= rows:
            return lat_in[1, row - rows]
        return react_ref[row]

    def circle_copy(row, step):
        target = lax.rem(lon + step, lons)
        return pltpu.make_async_remote_copy(
            src_ref=moved_ref.at[row, pl.ds(pl.multiple_of(target * share, share), share)],
            dst_ref=circle_ref.at[row, lon],
            send_sem=to_send.at[row, step], recv_sem=to_recv.at[row, step],
            device_id=(lat, target), device_id_type=MESH,
        )

    def back_copy(row, step):
        target = lax.rem(lon + step, lons)
        return pltpu.make_async_remote_copy(
            src_ref=result_ref.at[row, target],
            dst_ref=back_ref.at[row, pl.ds(pl.multiple_of(lon * share, share), share)],
            send_sem=from_send.at[row, step], recv_sem=from_recv.at[row, step],
            device_id=(lat, target), device_id_type=MESH,
        )

    own = pl.ds(pl.multiple_of(lon * share, share), share)
    south_flux = None
    step_below = line(-1) - line(-2)
    step_here = line(0) - line(-1)
    slope_low = minmod(step_below, step_here)
    for row in range(-1, rows):
        step_above = line(row + 2) - line(row + 1)
        slope_high = minmod(step_here, step_above)
        courant = meridional_in[rows - 1 :, :] if row < 0 else meridional_ref[row : row + 1, :]
        north_flux = flux(upwind(courant), line(row), slope_low, line(row + 1), slope_high)
        if row >= 0:
            weights = table_ref[lat, row : row + 1, total_lon:]
            moved = moved_ref[row] - (
                weights[:, 0:1] * north_flux - weights[:, 1:2] * south_flux
            )
            moved_ref[row] = moved
            out_ref[pl.ds(row, species, stride=rows), :] = moved

            @pl.when(polar)
            def _(row=row):
                for step in range(1, lons):
                    circle_copy(row, step).start()
                circle_ref[row, lon] = moved_ref[row, own]

        south_flux = north_flux
        slope_low = slope_high
        step_here = step_above

    @pl.when(polar)
    def _():
        for row in range(rows):
            taps = table_ref[lat, row : row + 1, :total_lon]
            taps = taps * flag_ref[row].astype(jnp.float32)
            spread = pltpu.roll(
                jnp.broadcast_to(taps, (cells, total_lon)), 0, 1, stride=1, stride_axis=0
            )
            spread_high, spread_low = split(spread)
            for step in range(1, lons):
                circle_copy(row, step).wait_recv()
            signal = circle_ref[row].reshape(species, cells)
            high, low = split(signal)
            product = (
                times(high, spread_high) + times(low, spread_high) + times(high, spread_low)
            )
            for target in range(lons):
                value = signal[target * share : (target + 1) * share]
                for source in range(lons):
                    offset = (target - source) % lons * cells
                    value -= product[
                        source * share : (source + 1) * share, offset : offset + cells
                    ]
                result_ref[row, target] = value
            for step in range(1, lons):
                back_copy(row, step).start()
            back_ref[row, own] = result_ref[row, lon]
        for row in range(rows):
            for step in range(1, lons):
                back_copy(row, step).wait_recv()
            out_ref[pl.ds(row, species, stride=rows), :] = back_ref[row]
        for row in range(rows):
            for step in range(1, lons):
                circle_copy(row, step).wait_send()
                back_copy(row, step).wait_send()

    for copy in edge_copies:
        copy.wait_send()

    @pl.when(has_north)
    def _():
        lat_copies[0].wait_send()
        wall_copy.wait_send()

    @pl.when(has_south)
    def _():
        lat_copies[1].wait_send()


def transport(lats, lons, reacted, zonal, meridional, table, flags):
    rows, species, cells = reacted.shape
    share = species // lons
    vmem = pl.BlockSpec(memory_space=pltpu.VMEM)
    real = jnp.float32
    dma = pltpu.SemaphoreType.DMA
    return pl.pallas_call(
        functools.partial(transport_kernel, lats, lons),
        out_shape=jax.ShapeDtypeStruct((rows * species, cells), real),
        in_specs=[vmem] * 4 + [pl.BlockSpec(memory_space=pltpu.SMEM)],
        out_specs=vmem,
        scratch_shapes=[
            pltpu.VMEM((2, rows + 1, 8, cells), real),
            pltpu.VMEM((2, rows + 1, 8, cells), real),
            pltpu.VMEM((2, 2, species, cells), real),
            pltpu.VMEM((rows, cells), real),
            pltpu.VMEM((rows, species, cells), real),
            pltpu.VMEM((rows, lons, share, cells), real),
            pltpu.VMEM((rows, lons, share, cells), real),
            pltpu.VMEM((rows, species, cells), real),
            dma((2,)), dma((2,)), dma((2,)), dma((2,)), dma, dma,
            dma((rows, lons)), dma((rows, lons)), dma((rows, lons)), dma((rows, lons)),
        ],
        compiler_params=pltpu.CompilerParams(
            collective_id=0, has_side_effects=True, vmem_limit_bytes=24 * 1024 * 1024
        ),
    )(reacted, zonal, meridional, table, flags)


def per_device(
    species_density,
    zonal_wall_ratio,
    meridional_wall_ratio,
    normalized_warmth,
    kinetic_coefficient,
    thermal_exponent,
    product_amounts,
    reagent_pairs,
    inner_iterations,
    smoothed_parallel_flags,
):
    species, level_list, lat_rows, meridian_boxes = species_density.shape
    lat_devices = lax.axis_size("lat")
    lon_devices = lax.axis_size("lon")
    reacted = react(
        species_density.reshape(species * lat_rows, meridian_boxes),
        normalized_warmth.reshape(lat_rows, meridian_boxes),
        kinetic_coefficient.reshape(1, -1),
        thermal_exponent.reshape(1, -1),
        product_amounts,
        reagent_pairs,
        inner_iterations.reshape(lat_rows),
    )
    table = row_tables(lat_rows * lat_devices, meridian_boxes * lon_devices)
    filtered = transport(
        lat_devices,
        lon_devices,
        reacted,
        zonal_wall_ratio.reshape(lat_rows, meridian_boxes),
        meridional_wall_ratio.reshape(lat_rows, meridian_boxes),
        jnp.asarray(table).reshape(lat_devices, lat_rows, -1),
        smoothed_parallel_flags,
    )
    return filtered.reshape(species, level_list, lat_rows, meridian_boxes)


def solution(mesh):
    placed = (
        P(None, None, "lat", "lon"),
        P(None, "lat", "lon"),
        P(None, "lat", "lon"),
        P(None, "lat", "lon"),
        P(),
        P(),
        P(),
        P(),
        P(None, "lat", "lon"),
        P("lat"),
    )
    return jax.shard_map(
        per_device,
        mesh=mesh,
        in_specs=placed,
        out_specs=P(None, None, "lat", "lon"),
        check_vma=False,
    )
```

```python
import functools
import math

import jax
import jax.numpy as jnp
import numpy as np
from jax import lax
from jax.experimental import pallas as pl
from jax.experimental.pallas import tpu as pltpu
from jax.sharding import PartitionSpec as P

ITERS = 2
chunk = 256
group = 2
chem_vmem = 56 * 1024 * 1024


chem_step = 1.0
polar_cut = 0.5


def split(value):
    high = value.astype(jnp.bfloat16)
    low = (value - high.astype(jnp.float32)).astype(jnp.bfloat16)
    return high, low


def times(left_val, right_val):
    return jnp.dot(left_val, right_val, preferred_element_type=jnp.float32)


def chem_kernel(
    count_ref, conc_hbm, warm_hbm, kinetic_hbm, thermal_hbm, product_hbm, pair_hbm, out_ref,
    conc_ref, warm_ref, kinetic_ref, thermal_ref, product_ref, pair_ref,
    gather_ref, collect_ref, rate_ref, state_ref, sems
):
    lat_rows, species, cells = out_ref.shape
    reac = pair_ref.shape[1]
    loads = [
        pltpu.make_async_copy(source, target, sems.at[i])
        for i, (source, target) in enumerate(
            (
                (pair_hbm, pair_ref),
                (kinetic_hbm, kinetic_ref),
                (thermal_hbm, thermal_ref),
                (warm_hbm, warm_ref),
                (product_hbm, product_ref),
                (conc_hbm, conc_ref),
            )
        )
    ]
    for load in loads:
        load.start()
    loads[0].wait()
    sub = lax.broadcasted_iota(jnp.int32, (species, reac), 0)
    used = jnp.zeros((species, reac), jnp.float32)
    for side in range(2):
        chosen = jnp.where(sub == pair_ref[side : side + 1, :], 1.0, 0.0).astype(jnp.float32)
        flipped = chosen.T.astype(jnp.bfloat16)
        gather_ref[pl.ds(side * reac, reac), :] = jnp.concatenate([flipped, flipped], 1)
        used += chosen
    collect_ref[species : 2 * species, :] = used.astype(jnp.bfloat16)
    for load in loads[1:4]:
        load.wait()
    kinetic = jnp.broadcast_to(kinetic_ref[...], (cells, reac)).T
    thermal = jnp.broadcast_to(thermal_ref[...], (cells, reac)).T
    for row in range(lat_rows):
        rate_ref[:, pl.ds(row * cells, cells)] = kinetic * jnp.exp(
            thermal * warm_ref[row : row + 1, :]
        )
    loads[4].wait()
    high, low = split(product_ref[...].T)
    collect_ref[:species, :] = high
    collect_ref[2 * species :, :] = low
    loads[5].wait()
    owner = lax.broadcasted_iota(jnp.int32, (1, lat_rows * cells), 1) // cells
    counts_all = jnp.full((1, lat_rows * cells), count_ref[0], jnp.int32)
    for row in range(lat_rows):
        counts_all = jnp.where(owner == row, count_ref[row], counts_all)
        state_ref[:, row * cells : (row + 1) * cells] = conc_ref[
            pl.ds(row, species, stride=lat_rows), :
        ]

    def turns_of(first_row):
        turns = count_ref[first_row]
        for row in range(first_row + 1, first_row + group):
            turns = jnp.maximum(turns, count_ref[row])
        return turns

    def run(first_row, size, begin, end):
        columns = slice(first_row * cells, (first_row + size) * cells)
        counts = counts_all[:, columns]
        step_len = chem_step / counts.astype(jnp.float32)

        def advance_once(index, carry):
            start_conc = state_ref[:, columns]
            amounts = start_conc
            for sweep in range(ITERS):
                stacked = jnp.concatenate(split(amounts), 0)
                produced = jnp.zeros_like(start_conc)
                lost = jnp.zeros_like(start_conc)
                for part in range(0, reac, chunk):
                    reactions = pl.ds(part, chunk)
                    first_conc = times(gather_ref[reactions, :], stacked)
                    second = times(gather_ref[pl.ds(reac + part, chunk), :], stacked)
                    made = rate_ref[reactions, columns] * first_conc * second
                    made_high, made_low = split(made)
                    main = times(collect_ref[:, reactions], made_high)
                    rest = times(collect_ref[: 2 * species, reactions], made_low)
                    produced += main[:species] + (main[2 * species :] + rest[:species])
                    lost += main[species : 2 * species] + rest[species:]
                loss_rate = lost / amounts
                amounts = (start_conc + step_len * produced) / (1.0 + step_len * loss_rate)
            state_ref[:, columns] = jnp.where(counts > index, amounts, start_conc)
            return carry

        lax.fori_loop(begin, end, advance_once, 0)

    groups = range(0, lat_rows, group)
    together = turns_of(0)
    for first_row in groups:
        together = jnp.minimum(together, turns_of(first_row))
    run(0, lat_rows, 0, together)
    for first_row in groups:
        run(first_row, group, together, turns_of(first_row))
    for row in range(lat_rows):
        out_ref[row] = state_ref[:, row * cells : (row + 1) * cells]


def react(conc, warm, kinetic, thermal, product, pairs, counts):
    species = product.shape[1]
    reac = product.shape[0]
    lat_rows, cells = warm.shape
    operands = (conc, warm, kinetic, thermal, product, pairs)
    anywhere = pl.BlockSpec(memory_space=pl.ANY)
    return pl.pallas_call(
        chem_kernel,
        out_shape=jax.ShapeDtypeStruct((lat_rows, species, cells), jnp.float32),
        in_specs=[pl.BlockSpec(memory_space=pltpu.SMEM)] + [anywhere] * len(operands),
        out_specs=pl.BlockSpec(memory_space=pltpu.VMEM),
        scratch_shapes=[pltpu.VMEM(value.shape, value.dtype) for value in operands]
        + [
            pltpu.VMEM((2 * reac, 2 * species), jnp.bfloat16),
            pltpu.VMEM((3 * species, reac), jnp.bfloat16),
            pltpu.VMEM((reac, lat_rows * cells), jnp.float32),
            pltpu.VMEM((species, lat_rows * cells), jnp.float32),
            pltpu.SemaphoreType.DMA((len(operands),)),
        ],
        compiler_params=pltpu.CompilerParams(vmem_limit_bytes=chem_vmem),
    )(counts, *operands)


def minmod(left_val, right_val):
    return jnp.maximum(0.0, jnp.minimum(left_val, right_val)) + jnp.minimum(
        0.0, jnp.maximum(left_val, right_val)
    )


MESH = pl.DeviceIdType.MESH


def row_tables(total_rows, total_lon):
    faces = np.arange(total_rows + 1) * (math.pi / total_rows) - math.pi / 2
    centres = (np.arange(total_rows) + 0.5) * (math.pi / total_rows) - math.pi / 2
    modes = np.arange(1, total_lon // 2 + 1)
    ratio = np.cos(centres) / polar_cut
    keep = np.minimum(1.0, ratio[:, None] / np.sin(modes[None, :] * (math.pi / total_lon)))
    damp = np.concatenate([np.zeros((total_rows, 1)), 1.0 - keep], 1)
    taps = np.fft.irfft(damp, n=total_lon, axis=1)
    weights = np.zeros((total_rows, 128))
    weights[:, 0] = np.cos(faces[1:]) / np.cos(centres)
    weights[:, 1] = np.cos(faces[:-1]) / np.cos(centres)
    return np.concatenate([taps, weights], 1).astype(np.float32)


def upwind(courant):
    plus = jnp.maximum(courant, 0.0)
    minus = jnp.minimum(courant, 0.0)
    return plus, 0.5 * plus * (1.0 - courant), minus, 0.5 * minus * (1.0 + courant)


def flux(parts, low, low_slope, high, high_slope):
    plus, plus_slope, minus, minus_slope = parts
    return (plus * low + plus_slope * low_slope) + (minus * high - minus_slope * high_slope)


def transport_kernel(
    lats, lons, react_ref, zonal_ref, meridional_ref, table_ref, flag_ref, out_ref,
    edge_ref, edge_in, lat_in, meridional_in, moved_ref, circle_ref, result_ref, back_ref,
    edge_send, edge_recv, lat_send, lat_recv, wall_send, wall_recv,
    to_send, to_recv, from_send, from_recv
):
    rows, species, cells = react_ref.shape
    share = species // lons
    total_lon = lons * cells
    lat = lax.axis_index("lat")
    lon = lax.axis_index("lon")
    has_north = lat < lats - 1
    has_south = lat > 0
    quarter = lats // 4
    polar = jnp.logical_or(lat < quarter, lat >= lats - quarter)

    far_first = sorted(range(1, lons), key=lambda step: -min(step, lons - step))
    barrier = pltpu.get_barrier_semaphore()
    for step in range(1, lons):
        pl.semaphore_signal(
            barrier, inc=1, device_id=(lat, lax.rem(lon + step, lons)), device_id_type=MESH
        )

    @pl.when(has_north)
    def _():
        pl.semaphore_signal(barrier, inc=1, device_id=(lat + 1, lon), device_id_type=MESH)

    @pl.when(has_south)
    def _():
        pl.semaphore_signal(barrier, inc=1, device_id=(lat - 1, lon), device_id_type=MESH)

    for row in range(rows):
        turned = react_ref[row].T
        edge_ref[0, row] = turned[cells - 8 :]
        edge_ref[1, row] = turned[:8]
    edge_ref[0, rows, :rows] = zonal_ref[...]
    edge_ref[1, rows, :rows] = zonal_ref[...]

    @pl.when(jnp.logical_not(has_south))
    def _():
        lat_in[0] = jnp.zeros((2, species, cells), jnp.float32)
        meridional_in[...] = jnp.zeros((rows, cells), jnp.float32)

    @pl.when(jnp.logical_not(has_north))
    def _():
        lat_in[1] = jnp.zeros((2, species, cells), jnp.float32)

    neighbours = lons - 1 + has_north.astype(jnp.int32) + has_south.astype(jnp.int32)
    pl.semaphore_wait(barrier, neighbours)

    def edge_copy(side):
        target = lax.rem(lon + 1, lons) if side == 0 else lax.rem(lon + lons - 1, lons)
        return pltpu.make_async_remote_copy(
            src_ref=edge_ref.at[side], dst_ref=edge_in.at[side],
            send_sem=edge_send.at[side], recv_sem=edge_recv.at[side],
            device_id=(lat, target), device_id_type=MESH,
        )

    def lat_copy(side):
        first = rows - 2 if side == 0 else 0
        return pltpu.make_async_remote_copy(
            src_ref=react_ref.at[pl.ds(first, 2)], dst_ref=lat_in.at[side],
            send_sem=lat_send.at[side], recv_sem=lat_recv.at[side],
            device_id=(lat + 1 if side == 0 else lat - 1, lon), device_id_type=MESH,
        )

    wall_copy = pltpu.make_async_remote_copy(
        src_ref=meridional_ref, dst_ref=meridional_in,
        send_sem=wall_send, recv_sem=wall_recv,
        device_id=(lat + 1, lon), device_id_type=MESH,
    )
    edge_copies = [edge_copy(0), edge_copy(1)]
    lat_copies = [lat_copy(0), lat_copy(1)]
    for copy in edge_copies:
        copy.start()

    @pl.when(has_north)
    def _():
        lat_copies[0].start()
        wall_copy.start()

    @pl.when(has_south)
    def _():
        lat_copies[1].start()

    for copy in edge_copies:
        copy.wait_recv()

    lane = lax.broadcasted_iota(jnp.int32, (1, cells), 1)
    gap = jnp.zeros((cells - 16, species), jnp.float32)
    for row in range(rows):
        here = react_ref[row]
        outside = jnp.concatenate([edge_in[1, row], gap, edge_in[0, row]], 0).T
        west = pltpu.roll(jnp.where(lane == cells - 1, outside, here), 1, 1)
        west_two = pltpu.roll(jnp.where(lane >= cells - 2, outside, here), 2, 1)
        east = pltpu.roll(jnp.where(lane == 0, outside, here), cells - 1, 1)
        east_two = pltpu.roll(jnp.where(lane < 2, outside, here), cells - 2, 1)
        west_step = here - west
        east_step = east - here
        slope = minmod(west_step, east_step)
        west_slope = minmod(west - west_two, west_step)
        east_slope = minmod(east_step, east_two - east)
        courant = zonal_ref[row : row + 1, :]
        courant_west = pltpu.roll(
            jnp.where(lane == cells - 1, edge_in[0, rows, row : row + 1, :], courant), 1, 1
        )
        leaving = flux(upwind(courant), here, slope, east, east_slope)
        entering = flux(upwind(courant_west), west, west_slope, here, slope)
        moved_ref[row] = here - (leaving - entering)

    @pl.when(has_south)
    def _():
        lat_copies[0].wait_recv()
        wall_copy.wait_recv()

    @pl.when(has_north)
    def _():
        lat_copies[1].wait_recv()

    def line(row):
        if row < 0:
            return lat_in[0, row + 2]
        if row >= rows:
            return lat_in[1, row - rows]
        return react_ref[row]

    def circle_copy(row, step):
        target = lax.rem(lon + step, lons)
        return pltpu.make_async_remote_copy(
            src_ref=moved_ref.at[row, pl.ds(pl.multiple_of(target * share, share), share)],
            dst_ref=circle_ref.at[row, lon],
            send_sem=to_send.at[row, step], recv_sem=to_recv.at[row, step],
            device_id=(lat, target), device_id_type=MESH,
        )

    def back_copy(row, step):
        target = lax.rem(lon + step, lons)
        return pltpu.make_async_remote_copy(
            src_ref=result_ref.at[row, target],
            dst_ref=back_ref.at[row, pl.ds(pl.multiple_of(lon * share, share), share)],
            send_sem=from_send.at[row, step], recv_sem=from_recv.at[row, step],
            device_id=(lat, target), device_id_type=MESH,
        )

    own = pl.ds(pl.multiple_of(lon * share, share), share)
    south_flux = None
    step_below = line(-1) - line(-2)
    step_here = line(0) - line(-1)
    slope_low = minmod(step_below, step_here)
    for row in range(-1, rows):
        step_above = line(row + 2) - line(row + 1)
        slope_high = minmod(step_here, step_above)
        courant = meridional_in[rows - 1 :, :] if row < 0 else meridional_ref[row : row + 1, :]
        north_flux = flux(upwind(courant), line(row), slope_low, line(row + 1), slope_high)
        if row >= 0:
            weights = table_ref[lat, row : row + 1, total_lon:]
            moved = moved_ref[row] - (
                weights[:, 0:1] * north_flux - weights[:, 1:2] * south_flux
            )
            moved_ref[row] = moved
            out_ref[pl.ds(row, species, stride=rows), :] = moved

            @pl.when(polar)
            def _(row=row):
                for step in far_first:
                    circle_copy(row, step).start()
                circle_ref[row, lon] = moved_ref[row, own]

        south_flux = north_flux
        slope_low = slope_high
        step_here = step_above

    @pl.when(polar)
    def _():
        for row in range(rows):
            taps = table_ref[lat, row : row + 1, :total_lon]
            taps = taps * flag_ref[row].astype(jnp.float32)
            spread = pltpu.roll(
                jnp.broadcast_to(taps, (cells, total_lon)), 0, 1, stride=1, stride_axis=0
            )
            spread_high, spread_low = split(spread)
            for step in range(1, lons):
                circle_copy(row, step).wait_recv()
            signal = circle_ref[row].reshape(species, cells)
            high, low = split(signal)
            product = (
                times(high, spread_high) + times(low, spread_high) + times(high, spread_low)
            )
            for target in range(lons):
                value = signal[target * share : (target + 1) * share]
                for source in range(lons):
                    offset = (target - source) % lons * cells
                    value -= product[
                        source * share : (source + 1) * share, offset : offset + cells
                    ]
                result_ref[row, target] = value
            for step in far_first:
                back_copy(row, step).start()
            back_ref[row, own] = result_ref[row, lon]
        for row in range(rows):
            for step in range(1, lons):
                back_copy(row, step).wait_recv()
            out_ref[pl.ds(row, species, stride=rows), :] = back_ref[row]
        for row in range(rows):
            for step in range(1, lons):
                circle_copy(row, step).wait_send()
                back_copy(row, step).wait_send()

    for copy in edge_copies:
        copy.wait_send()

    @pl.when(has_north)
    def _():
        lat_copies[0].wait_send()
        wall_copy.wait_send()

    @pl.when(has_south)
    def _():
        lat_copies[1].wait_send()


def transport(lats, lons, reacted, zonal, meridional, table, flags):
    rows, species, cells = reacted.shape
    share = species // lons
    vmem = pl.BlockSpec(memory_space=pltpu.VMEM)
    real = jnp.float32
    dma = pltpu.SemaphoreType.DMA
    return pl.pallas_call(
        functools.partial(transport_kernel, lats, lons),
        out_shape=jax.ShapeDtypeStruct((rows * species, cells), real),
        in_specs=[vmem] * 4 + [pl.BlockSpec(memory_space=pltpu.SMEM)],
        out_specs=vmem,
        scratch_shapes=[
            pltpu.VMEM((2, rows + 1, 8, cells), real),
            pltpu.VMEM((2, rows + 1, 8, cells), real),
            pltpu.VMEM((2, 2, species, cells), real),
            pltpu.VMEM((rows, cells), real),
            pltpu.VMEM((rows, species, cells), real),
            pltpu.VMEM((rows, lons, share, cells), real),
            pltpu.VMEM((rows, lons, share, cells), real),
            pltpu.VMEM((rows, species, cells), real),
            dma((2,)), dma((2,)), dma((2,)), dma((2,)), dma, dma,
            dma((rows, lons)), dma((rows, lons)), dma((rows, lons)), dma((rows, lons)),
        ],
        compiler_params=pltpu.CompilerParams(
            collective_id=0, has_side_effects=True, vmem_limit_bytes=24 * 1024 * 1024
        ),
    )(reacted, zonal, meridional, table, flags)


def per_device(
    species_density,
    zonal_wall_ratio,
    meridional_wall_ratio,
    normalized_warmth,
    kinetic_coefficient,
    thermal_exponent,
    product_amounts,
    reagent_pairs,
    inner_iterations,
    smoothed_parallel_flags,
):
    species, level_list, lat_rows, meridian_boxes = species_density.shape
    lat_devices = lax.axis_size("lat")
    lon_devices = lax.axis_size("lon")
    reacted = react(
        species_density.reshape(species * lat_rows, meridian_boxes),
        normalized_warmth.reshape(lat_rows, meridian_boxes),
        kinetic_coefficient.reshape(1, -1),
        thermal_exponent.reshape(1, -1),
        product_amounts,
        reagent_pairs,
        inner_iterations.reshape(lat_rows),
    )
    table = row_tables(lat_rows * lat_devices, meridian_boxes * lon_devices)
    filtered = transport(
        lat_devices,
        lon_devices,
        reacted,
        zonal_wall_ratio.reshape(lat_rows, meridian_boxes),
        meridional_wall_ratio.reshape(lat_rows, meridian_boxes),
        jnp.asarray(table).reshape(lat_devices, lat_rows, -1),
        smoothed_parallel_flags,
    )
    return filtered.reshape(species, level_list, lat_rows, meridian_boxes)


def solution(mesh):
    placed = (
        P(None, None, "lat", "lon"),
        P(None, "lat", "lon"),
        P(None, "lat", "lon"),
        P(None, "lat", "lon"),
        P(),
        P(),
        P(),
        P(),
        P(None, "lat", "lon"),
        P("lat"),
    )
    return jax.shard_map(
        per_device,
        mesh=mesh,
        in_specs=placed,
        out_specs=P(None, None, "lat", "lon"),
        check_vma=False,
    )
```
